32 devices in a mesh: grp: 2 (over y), tm: 16 (over z, x, core).
Axes of the slice: x: 2, y: 2, z: 4, core: 2. Of those that a mesh axis runs over, the one named last changes fastest.
Arguments:
- residual: bfloat16 [4, 2, 4096, 2048], P('grp', None, 'tm'), parts along dimension 0, may hold values from -6 to 6
- eigenbasis: bfloat16 [2048, 2048], P('tm'), may hold values from -0.125 to 0.125
- eigenvalues: float32 [2048], replicated, may hold values from 0.05 to 5
- node_order: int32 [2048], replicated, may hold values from 0 to 2047, each once
Outputs:
- correction: float32 [4, 2, 4096, 2048], P('grp', None, 'tm'), parts along dimension 0
The draws below stay inside these ranges and needn't reach their ends.
There are 2 independent parts, one for each index of `grp`. The reference program is written for one: setup_inputs(seed, part) draws one part's arguments, and reference() takes and returns one part's arrays. A program takes and returns all parts, laid end to end along the dimension named above; an argument that names none is the same for every part. Nothing has to cross between parts.
Inputs may be any that keep to these rules, and one draw needn't show every extreme that they name: node_order names every number of 0 to 2047 exactly once.
All inputs are finite; a program needn't handle non-finite values.
Results may differ from the reference program's by a relative error of at most 0.0055.
Values may be sent and summed in bfloat16 or wider, within the bound.
A program may use at most 64 MiB of HBM per device.

```python
import math
import jax
import jax.numpy as jnp

NT = 4096
NS = 2048
FIELDS = 2
RHS = 2


def levels(stream_key, extent, split, low, top_value):
    gain, own = 1.0, jax.random.fold_in(stream_key, 6)
    for axis_at, blocks in split:
        steps = jnp.exp(jax.random.uniform(jax.random.fold_in(own, axis_at), (blocks,), jnp.float32, low / len(split), top_value / len(split)))
        gain = gain * jnp.repeat(steps, extent[axis_at] // blocks).reshape([-1 if axis == axis_at else 1 for axis in range(len(extent))])
    return gain


def gaussian(rng, dims, scale, bound, cuts=(), kind=jnp.bfloat16):
    level = levels(rng, dims, cuts, -0.22, 0.18) if cuts else 1.0
    array = jax.random.normal(rng, dims, jnp.float32) * scale * level
    return jnp.minimum(jnp.maximum(array, -bound), bound).astype(kind)


def setup_inputs(seed: int = 0, part: int = 0) -> dict:
    key_of = jax.random.split(jax.random.key(seed), 5)
    own_keys = jax.random.split(jax.random.fold_in(key_of[4], part), 5)
    residual = gaussian(own_keys[0], (RHS, FIELDS, NT, NS), 1.0, 6.0, ((2, 16),))
    eigenbasis = gaussian(key_of[1], (NS, NS), NS ** -0.5, 0.125, ((0, 16),))
    eigenvalues = jnp.clip(jnp.exp(jax.random.uniform(key_of[2], (NS,), jnp.float32, math.log(0.05), math.log(5.0))), 0.05, 5.0)
    node_order = jax.random.permutation(key_of[3], NS).astype(jnp.int32)
    return dict(residual=residual, eigenbasis=eigenbasis, eigenvalues=eigenvalues, node_order=node_order)


def sine_block(length, first_col, block_width):
    row_index = jnp.arange(length, dtype=jnp.int32)[:, None] + 1
    col_index = first_col + jnp.arange(block_width, dtype=jnp.int32)[None, :] + 1
    phase_mod = row_index * col_index % (2 * (length + 1))
    angle_rad = phase_mod.astype(jnp.float32) * (jnp.pi / (length + 1))
    return (jnp.sqrt(2.0 / (length + 1)) * jnp.sin(angle_rad)).astype(jnp.bfloat16)

def reference(residual, eigenbasis, eigenvalues, node_order):
    ordered = jnp.take(residual, node_order, axis=3)
    modal_data = jnp.einsum('sj,rfts->rfjt', eigenbasis.astype(jnp.float32), ordered.astype(jnp.float32)).astype(jnp.bfloat16)
    sine_table = sine_block(NT, 0, NT)
    flat_modal = modal_data.reshape(-1, NT)
    spectral = jnp.dot(flat_modal, sine_table, preferred_element_type=jnp.float32).reshape(RHS, FIELDS, NS, NT)
    freq_index = (jnp.arange(NT, dtype=jnp.int32) + 1).astype(jnp.float32)
    time_eigen = 4.0 * jnp.sin(freq_index * (jnp.pi / (2 * (NT + 1)))) ** 2
    shift_sum = eigenvalues[:, None] + time_eigen[None, :]
    determinant = shift_sum * shift_sum + 1.0
    state_part = (shift_sum * spectral[:, 0] - spectral[:, 1]) / determinant
    adjoint = (spectral[:, 0] + shift_sum * spectral[:, 1]) / determinant
    scaled = jnp.stack((state_part, adjoint), axis=1).astype(jnp.bfloat16)
    back_modes = jnp.dot(scaled.reshape(-1, NT), sine_table.T, preferred_element_type=jnp.float32)
    back_modes = back_modes.astype(jnp.bfloat16).reshape(RHS, FIELDS, NS, NT)
    shaped = jnp.einsum('sj,rfjt->rfts', eigenbasis.astype(jnp.float32), back_modes.astype(jnp.float32))
    correction = jnp.zeros(shaped.shape, jnp.float32).at[:, :, :, node_order].set(shaped)
    return correction
```

```python
import functools

import jax
import jax.numpy as jnp
from jax import lax
from jax.experimental import pallas as pl
from jax.experimental.pallas import tpu as pltpu
from jax.sharding import PartitionSpec as P

SEGMENTS = 8


def mul(a, b):
    return a[0] * b[0] - a[1] * b[1], a[0] * b[1] + a[1] * b[0]


def add(a, b):
    return a[0] + b[0], a[1] + b[1]


def sub(a, b):
    return a[0] - b[0], a[1] - b[1]


def inverse_of(a):
    size = a[0] * a[0] + a[1] * a[1]
    return a[0] / size, -a[1] / size


def power(a, exponent):
    result, square = None, a
    while exponent:
        if exponent & 1:
            result = square if result is None else mul(result, square)
        exponent >>= 1
        if exponent:
            square = mul(square, square)
    return result


def decay_root(mu):
    wide = 2.0 + mu
    disc_re, disc_im = wide * wide - 5.0, -2.0 * wide
    size = jnp.sqrt(disc_re * disc_re + disc_im * disc_im)
    sqrt_re = jnp.sqrt(0.5 * (size + disc_re))
    sqrt_im = 0.5 * disc_im / sqrt_re
    half = inverse_of((wide + sqrt_re, sqrt_im - 1.0))
    return 2.0 * half[0], 2.0 * half[1]


def carries_kernel(modal_ref, mu_ref, perm_ref, zp_ref, seg_ref, dev_ref, z_ref):
    vectors, _, steps, width = modal_ref.shape
    per_seg = steps // SEGMENTS
    root = decay_root(mu_ref[...])
    root8 = tuple(jnp.broadcast_to(x, (SEGMENTS, width)) for x in root)
    jump = power(root, per_seg)
    for r in range(vectors):
        for f in range(2):
            rows = jnp.dot(perm_ref[...], modal_ref[r, f], preferred_element_type=jnp.float32)
            z_ref[r, f] = rows
            zp_ref[r, f] = rows.astype(jnp.bfloat16)
    for r in range(vectors):
        def at(k):
            here = pl.ds(k * SEGMENTS, SEGMENTS)
            return z_ref[r, 0, here, :], z_ref[r, 1, here, :]

        ahead, behind = at(0), at(per_seg - 1)
        for k in range(1, per_seg):
            ahead = add(at(k), mul(root8, ahead))
            behind = add(at(per_seg - 1 - k), mul(root8, behind))
        for c in range(2):
            seg_ref[r, 0, c] = ahead[c]
            seg_ref[r, 1, c] = behind[c]
        row = lambda a, s: (a[0][s:s + 1], a[1][s:s + 1])
        front, back = row(ahead, 0), row(behind, SEGMENTS - 1)
        for s in range(1, SEGMENTS):
            front = add(row(ahead, s), mul(jump, front))
            back = add(row(behind, SEGMENTS - 1 - s), mul(jump, back))
        for c in range(2):
            dev_ref[r, 0, c] = front[c]
            dev_ref[r, 1, c] = back[c]


def solve_kernel(zp_ref, seg_ref, edge_ref, mu_ref, perm_ref, out_ref, p_ref, u_ref):
    vectors, _, steps, width = zp_ref.shape
    per_seg = steps // SEGMENTS
    root = decay_root(mu_ref[...])
    root8 = tuple(jnp.broadcast_to(x, (SEGMENTS, width)) for x in root)
    jump = power(root, per_seg)
    square = mul(root, root)
    gain = mul(root, inverse_of((1.0 - square[0], -square[1])))
    for r in range(vectors):
        row = lambda a, s: (seg_ref[r, a, 0, s:s + 1, :], seg_ref[r, a, 1, s:s + 1, :])
        lefts = [(edge_ref[r, 0, 0], edge_ref[r, 0, 1])]
        rights = [(edge_ref[r, 1, 0], edge_ref[r, 1, 1])]
        for s in range(SEGMENTS):
            lefts.append(add(row(0, s), mul(jump, lefts[-1])))
        for s in range(SEGMENTS - 1, 0, -1):
            rights.append(add(row(1, s), mul(jump, rights[-1])))
        rights = rights[::-1]
        ends = [mul(gain, add(rights[s], mul(root, lefts[s + 1]))) for s in range(SEGMENTS)]
        stack = lambda rows: tuple(jnp.concatenate([x[c] for x in rows], axis=0) for c in range(2))
        p = stack(lefts[:SEGMENTS])
        for k in range(0, per_seg, 2):
            both = pl.ds(k * SEGMENTS, 2 * SEGMENTS)
            pair = [zp_ref[r, f, both, :].astype(jnp.float32) for f in range(2)]
            for h in range(2):
                z = tuple(x[h * SEGMENTS:(h + 1) * SEGMENTS] for x in pair)
                p = add(z, mul(root8, p))
                for c in range(2):
                    p_ref[c, pl.ds((k + h) * SEGMENTS, SEGMENTS), :] = p[c]
        u = stack(ends)
        for k in range(per_seg - 2, -1, -2):
            later = []
            for h in (1, 0):
                here = pl.ds((k + h) * SEGMENTS, SEGMENTS)
                u = mul(root8, add((p_ref[0, here, :], p_ref[1, here, :]), u))
                later.append(u)
            both = pl.ds(k * SEGMENTS, 2 * SEGMENTS)
            for c in range(2):
                u_ref[c, both, :] = jnp.concatenate([later[1][c], later[0][c]], axis=0).astype(jnp.bfloat16)
        for c in range(2):
            out_ref[r, c] = jnp.dot(perm_ref[...], u_ref[c], preferred_element_type=jnp.float32).astype(jnp.bfloat16)


def on_device(residual, eigenbasis, eigenvalues, node_order):
    vectors, fields, steps, states = residual.shape
    modes = eigenbasis.shape[1]
    parts = lax.axis_size("tm")
    me = lax.axis_index("tm")
    per_seg = steps // SEGMENTS
    width = min(256, modes)
    blocks = modes // width

    inverse = jnp.zeros_like(node_order).at[node_order].set(jnp.arange(states, dtype=jnp.int32), unique_indices=True)
    basis = lax.all_gather(eigenbasis, "tm", axis=0, tiled=True)
    basis = jnp.take(basis, inverse, axis=0, mode="clip", unique_indices=True)

    modal = jnp.einsum("rfts,sj->rftj", residual, basis, preferred_element_type=jnp.float32).astype(jnp.bfloat16)

    row = jnp.arange(steps, dtype=jnp.int32)
    time_of_row = (row % SEGMENTS) * per_seg + row // SEGMENTS
    perm = (time_of_row[:, None] == row[None, :]).astype(jnp.bfloat16)
    mu = eigenvalues[None, :]

    f32 = jnp.float32
    wide_block = pl.BlockSpec((vectors, fields, steps, width), lambda j: (0, 0, 0, j))
    seg_block = pl.BlockSpec((vectors, 2, 2, SEGMENTS, width), lambda j: (0, 0, 0, 0, j))
    dev_block = pl.BlockSpec((vectors, 2, 2, 1, width), lambda j: (0, 0, 0, 0, j))
    mu_block = pl.BlockSpec((1, width), lambda j: (0, j))
    perm_block = pl.BlockSpec((steps, steps), lambda j: (0, 0))
    params = pltpu.CompilerParams(vmem_limit_bytes=40 * 1024 * 1024)
    zp, seg, dev = pl.pallas_call(
        carries_kernel,
        grid=(blocks,),
        in_specs=[wide_block, mu_block, perm_block],
        out_specs=[wide_block, seg_block, dev_block],
        out_shape=[
            jax.ShapeDtypeStruct((vectors, fields, steps, modes), jnp.bfloat16),
            jax.ShapeDtypeStruct((vectors, 2, 2, SEGMENTS, modes), f32),
            jax.ShapeDtypeStruct((vectors, 2, 2, 1, modes), f32),
        ],
        scratch_shapes=[pltpu.VMEM((vectors, fields, steps, width), f32)],
        compiler_params=params,
        name="carries",
    )(modal, mu, perm)

    every = lax.all_gather(dev[:, :, :, 0, :], "tm", axis=0, tiled=False)
    root = decay_root(mu)
    hop = power(root, steps)
    zero = (jnp.zeros((vectors, modes), f32),) * 2
    pick = lambda keep, new, old: tuple(jnp.where(keep, a, b) for a, b in zip(new, old))
    left, right, all_left, all_right = zero, zero, zero, zero
    from_start = from_end = (jnp.ones_like(mu), jnp.zeros_like(mu))
    for d in range(parts):
        e = parts - 1 - d
        all_left = add((every[d, :, 0, 0], every[d, :, 0, 1]), mul(hop, all_left))
        all_right = add((every[e, :, 1, 0], every[e, :, 1, 1]), mul(hop, all_right))
        left = pick(d < me, all_left, left)
        right = pick(e > me, all_right, right)
        from_start = pick(d < me, mul(hop, from_start), from_start)
        from_end = pick(e > me, mul(hop, from_end), from_end)
    whole = mul(power(hop, parts), root)
    whole_sq = mul(whole, whole)
    scale = mul(root, inverse_of((1.0 - whole_sq[0], -whole_sq[1])))
    start_term = mul(scale, sub(all_right, mul(whole, all_left)))
    end_term = mul(scale, sub(all_left, mul(whole, all_right)))
    left = sub(left, mul(start_term, from_start))
    right = sub(right, mul(end_term, from_end))
    edge = jnp.stack((jnp.stack(left, 1), jnp.stack(right, 1)), 1)[:, :, :, None, :]

    back = pl.pallas_call(
        solve_kernel,
        grid=(blocks,),
        in_specs=[wide_block, seg_block, dev_block, mu_block, perm_block],
        out_specs=wide_block,
        out_shape=jax.ShapeDtypeStruct((vectors, fields, steps, modes), jnp.bfloat16),
        scratch_shapes=[
            pltpu.VMEM((2, steps, width), f32),
            pltpu.VMEM((2, steps, width), jnp.bfloat16),
        ],
        compiler_params=params,
        name="solve",
    )(zp, seg, edge, mu, perm.T)

    return jnp.einsum("rftj,sj->rfts", back, basis, preferred_element_type=jnp.float32)


def solution(mesh):
    placed = (P("grp", None, "tm", None), P("tm", None), P(), P())
    return jax.shard_map(
        on_device, mesh=mesh, in_specs=placed, out_specs=P("grp", None, "tm", None), check_vma=False
    )
```

```python
import functools

import jax
import jax.numpy as jnp
from jax import lax
from jax.experimental import pallas as pl
from jax.experimental.pallas import tpu as pltpu
from jax.sharding import PartitionSpec as P

SEGMENTS = 8


def mul(a, b):
    return a[0] * b[0] - a[1] * b[1], a[0] * b[1] + a[1] * b[0]


def add(a, b):
    return a[0] + b[0], a[1] + b[1]


def sub(a, b):
    return a[0] - b[0], a[1] - b[1]


def inverse_of(a):
    size = a[0] * a[0] + a[1] * a[1]
    return a[0] / size, -a[1] / size


def power(a, exponent):
    result, square = None, a
    while exponent:
        if exponent & 1:
            result = square if result is None else mul(result, square)
        exponent >>= 1
        if exponent:
            square = mul(square, square)
    return result


def decay_root(mu):
    wide = 2.0 + mu
    disc_re, disc_im = wide * wide - 5.0, -2.0 * wide
    size = jnp.sqrt(disc_re * disc_re + disc_im * disc_im)
    sqrt_re = jnp.sqrt(0.5 * (size + disc_re))
    sqrt_im = 0.5 * disc_im / sqrt_re
    half = inverse_of((wide + sqrt_re, sqrt_im - 1.0))
    return 2.0 * half[0], 2.0 * half[1]


def carries_kernel(modal_ref, mu_ref, perm_ref, zp_ref, seg_ref, dev_ref, z_ref):
    vectors, _, steps, width = modal_ref.shape
    per_seg = steps // SEGMENTS
    root = decay_root(mu_ref[...])
    root8 = tuple(jnp.broadcast_to(x, (SEGMENTS, width)) for x in root)
    jump = power(root, per_seg)
    for r in range(vectors):
        for f in range(2):
            rows = jnp.dot(perm_ref[...], modal_ref[r, f], preferred_element_type=jnp.float32)
            z_ref[r, f] = rows
            zp_ref[r, f] = rows.astype(jnp.bfloat16)
    for r in range(vectors):
        def at(k):
            here = pl.ds(k * SEGMENTS, SEGMENTS)
            return z_ref[r, 0, here, :], z_ref[r, 1, here, :]

        ahead, behind = at(0), at(per_seg - 1)
        for k in range(1, per_seg):
            ahead = add(at(k), mul(root8, ahead))
            behind = add(at(per_seg - 1 - k), mul(root8, behind))
        for c in range(2):
            seg_ref[r, 0, c] = ahead[c]
            seg_ref[r, 1, c] = behind[c]
        row = lambda a, s: (a[0][s:s + 1], a[1][s:s + 1])
        front, back = row(ahead, 0), row(behind, SEGMENTS - 1)
        for s in range(1, SEGMENTS):
            front = add(row(ahead, s), mul(jump, front))
            back = add(row(behind, SEGMENTS - 1 - s), mul(jump, back))
        for c in range(2):
            dev_ref[r, 0, c] = front[c]
            dev_ref[r, 1, c] = back[c]


def solve_kernel(zp_ref, seg_ref, edge_ref, mu_ref, perm_ref, out_ref, p_ref, u_ref):
    vectors, _, steps, width = zp_ref.shape
    per_seg = steps // SEGMENTS
    root = decay_root(mu_ref[...])
    root8 = tuple(jnp.broadcast_to(x, (SEGMENTS, width)) for x in root)
    jump = power(root, per_seg)
    square = mul(root, root)
    gain = mul(root, inverse_of((1.0 - square[0], -square[1])))
    for r in range(vectors):
        row = lambda a, s: (seg_ref[r, a, 0, s:s + 1, :], seg_ref[r, a, 1, s:s + 1, :])
        lefts = [(edge_ref[r, 0, 0], edge_ref[r, 0, 1])]
        rights = [(edge_ref[r, 1, 0], edge_ref[r, 1, 1])]
        for s in range(SEGMENTS):
            lefts.append(add(row(0, s), mul(jump, lefts[-1])))
        for s in range(SEGMENTS - 1, 0, -1):
            rights.append(add(row(1, s), mul(jump, rights[-1])))
        rights = rights[::-1]
        ends = [mul(gain, add(rights[s], mul(root, lefts[s + 1]))) for s in range(SEGMENTS)]
        stack = lambda rows: tuple(jnp.concatenate([x[c] for x in rows], axis=0) for c in range(2))
        p = stack(lefts[:SEGMENTS])
        for k in range(0, per_seg, 2):
            both = pl.ds(k * SEGMENTS, 2 * SEGMENTS)
            pair = [zp_ref[r, f, both, :].astype(jnp.float32) for f in range(2)]
            for h in range(2):
                z = tuple(x[h * SEGMENTS:(h + 1) * SEGMENTS] for x in pair)
                p = add(z, mul(root8, p))
                for c in range(2):
                    p_ref[c, pl.ds((k + h) * SEGMENTS, SEGMENTS), :] = p[c]
        u = stack(ends)
        for k in range(per_seg - 2, -1, -2):
            later = []
            for h in (1, 0):
                here = pl.ds((k + h) * SEGMENTS, SEGMENTS)
                u = mul(root8, add((p_ref[0, here, :], p_ref[1, here, :]), u))
                later.append(u)
            both = pl.ds(k * SEGMENTS, 2 * SEGMENTS)
            for c in range(2):
                u_ref[c, both, :] = jnp.concatenate([later[1][c], later[0][c]], axis=0).astype(jnp.bfloat16)
        for c in range(2):
            out_ref[r, c] = jnp.dot(perm_ref[...], u_ref[c], preferred_element_type=jnp.float32).astype(jnp.bfloat16)


def gather_kernel(chips, mine_ref, node_ref, out_ref, held, send_sem, recv_sem, pair_send, pair_recv):
    _, _, rows, modes = held.shape
    states = out_ref.shape[0]
    half = modes // 2
    tile = min(256, states)
    me = lax.axis_index("tm")
    core, chip = me % 2, me // 2
    odd = chip % 2
    place = (1 - odd) * (chip // 2) + odd * (chips - 1 - chip // 2)

    def chip_at(position):
        position = (position + chips) % chips
        second = position // (chips // 2)
        return (1 - second) * 2 * position + second * (2 * (chips - 1 - position) + 1)

    targets = (chip_at(place + 1) * 2 + core, chip_at(place - 1) * 2 + core)
    pair = chip * 2 + 1 - core

    def piece(step, h):
        source = chip_at(place - step if h == 0 else place + step)
        return source, held.at[source, core, :, pl.ds(h * half, half)]

    def ring(step, h):
        _, ref = piece(step, h)
        return pltpu.make_async_remote_copy(
            src_ref=ref, dst_ref=ref, send_sem=send_sem.at[step, h], recv_sem=recv_sem.at[step, h],
            device_id={"tm": targets[h]}, device_id_type=pl.DeviceIdType.MESH,
        )

    def share(step, h):
        _, ref = piece(step, h)
        return pltpu.make_async_remote_copy(
            src_ref=ref, dst_ref=ref, send_sem=pair_send.at[step, h], recv_sem=pair_recv.at[step, h],
            device_id={"tm": pair}, device_id_type=pl.DeviceIdType.MESH,
        )

    def place_rows(step, h, first):
        source, _ = piece(step, h)
        nodes = node_ref[source]
        columns = pl.ds(h * half, half)

        def one_tile(t, carry):
            start = pl.multiple_of(t * tile, tile)
            index = lax.broadcasted_iota(jnp.int32, (tile, 2 * rows), 0) + start
            choose = jnp.where(index == nodes, 1.0, 0.0).astype(jnp.bfloat16)
            block = held[source, :, :, columns].reshape(2 * rows, half)
            moved = jnp.dot(choose, block, preferred_element_type=jnp.float32)
            here = pl.ds(start, tile)
            if not first:
                moved = moved + out_ref[here, columns].astype(jnp.float32)
            out_ref[here, columns] = moved.astype(jnp.bfloat16)
            return carry

        lax.fori_loop(0, states // tile, one_tile, 0)

    held[chip, core] = mine_ref[...]
    barrier = pltpu.get_barrier_semaphore()
    for target in (*targets, pair):
        pl.semaphore_signal(barrier, inc=1, device_id={"tm": target}, device_id_type=pl.DeviceIdType.MESH)
    pl.semaphore_wait(barrier, 3)

    def one_step(step, first):
        for h in range(2):
            ring(step, h).start()
        for h in range(2):
            share(step, h).start()
        for h in range(2):
            share(step, h).wait()
            place_rows(step, h, first)
        for h in range(2):
            ring(step, h).wait()

    one_step(0, True)

    def body(step, carry):
        one_step(step, False)
        return carry

    lax.fori_loop(1, chips - 1, body, 0)
    for h in range(2):
        share(chips - 1, h).start()
    for h in range(2):
        share(chips - 1, h).wait()
        place_rows(chips - 1, h, False)


def on_device(residual, eigenbasis, eigenvalues, node_order):
    vectors, fields, steps, states = residual.shape
    modes = eigenbasis.shape[1]
    parts = lax.axis_size("tm")
    me = lax.axis_index("tm")
    per_seg = steps // SEGMENTS
    width = min(256, modes)
    blocks = modes // width

    chips = parts // 2
    rows = eigenbasis.shape[0]
    basis = pl.pallas_call(
        functools.partial(gather_kernel, chips),
        out_shape=jax.ShapeDtypeStruct((states, modes), jnp.bfloat16),
        in_specs=[pl.BlockSpec(memory_space=pltpu.VMEM)] * 2,
        out_specs=pl.BlockSpec(memory_space=pltpu.VMEM),
        scratch_shapes=[pltpu.VMEM((chips, 2, rows, modes), jnp.bfloat16)]
        + [pltpu.SemaphoreType.DMA((chips, 2))] * 4,
        compiler_params=pltpu.CompilerParams(
            collective_id=0, has_side_effects=True, vmem_limit_bytes=44 * 1024 * 1024
        ),
        name="gather_rows",
    )(eigenbasis, node_order.reshape(chips, 1, 2 * rows))

    modal = jnp.einsum("rfts,sj->rftj", residual, basis, preferred_element_type=jnp.float32).astype(jnp.bfloat16)

    row = jnp.arange(steps, dtype=jnp.int32)
    time_of_row = (row % SEGMENTS) * per_seg + row // SEGMENTS
    perm = (time_of_row[:, None] == row[None, :]).astype(jnp.bfloat16)
    mu = eigenvalues[None, :]

    f32 = jnp.float32
    wide_block = pl.BlockSpec((vectors, fields, steps, width), lambda j: (0, 0, 0, j))
    seg_block = pl.BlockSpec((vectors, 2, 2, SEGMENTS, width), lambda j: (0, 0, 0, 0, j))
    dev_block = pl.BlockSpec((vectors, 2, 2, 1, width), lambda j: (0, 0, 0, 0, j))
    mu_block = pl.BlockSpec((1, width), lambda j: (0, j))
    perm_block = pl.BlockSpec((steps, steps), lambda j: (0, 0))
    params = pltpu.CompilerParams(vmem_limit_bytes=40 * 1024 * 1024)
    zp, seg, dev = pl.pallas_call(
        carries_kernel,
        grid=(blocks,),
        in_specs=[wide_block, mu_block, perm_block],
        out_specs=[wide_block, seg_block, dev_block],
        out_shape=[
            jax.ShapeDtypeStruct((vectors, fields, steps, modes), jnp.bfloat16),
            jax.ShapeDtypeStruct((vectors, 2, 2, SEGMENTS, modes), f32),
            jax.ShapeDtypeStruct((vectors, 2, 2, 1, modes), f32),
        ],
        scratch_shapes=[pltpu.VMEM((vectors, fields, steps, width), f32)],
        compiler_params=params,
        name="carries",
    )(modal, mu, perm)

    root = decay_root(mu)
    hop = power(root, steps)
    one = (jnp.ones_like(mu), jnp.zeros_like(mu))
    zero = (jnp.zeros((vectors, modes), f32),) * 2
    pick = lambda keep, new, old: tuple(jnp.where(keep, a, b) for a, b in zip(new, old))
    group = dev[:, :, :, 0, :]
    left, right = zero, zero
    from_start, from_end, span, reach = one, one, hop, 1
    while reach < parts:
        other = lax.ppermute(group, "tm", [(d, d ^ reach) for d in range(parts)])
        upper = (me // reach) % 2 == 1
        low, high = jnp.where(upper, other, group), jnp.where(upper, group, other)
        low_front, high_front = (low[:, 0, 0], low[:, 0, 1]), (high[:, 0, 0], high[:, 0, 1])
        low_back, high_back = (low[:, 1, 0], low[:, 1, 1]), (high[:, 1, 0], high[:, 1, 1])
        left = pick(upper, add(left, mul(from_start, low_front)), left)
        right = pick(upper, right, add(right, mul(from_end, high_back)))
        from_start = pick(upper, mul(from_start, span), from_start)
        from_end = pick(upper, from_end, mul(from_end, span))
        front, back = add(high_front, mul(span, low_front)), add(low_back, mul(span, high_back))
        group = jnp.stack((jnp.stack(front, 1), jnp.stack(back, 1)), 1)
        span, reach = mul(span, span), 2 * reach
    all_left, all_right = (group[:, 0, 0], group[:, 0, 1]), (group[:, 1, 0], group[:, 1, 1])
    whole = mul(span, root)
    whole_sq = mul(whole, whole)
    scale = mul(root, inverse_of((1.0 - whole_sq[0], -whole_sq[1])))
    start_term = mul(scale, sub(all_right, mul(whole, all_left)))
    end_term = mul(scale, sub(all_left, mul(whole, all_right)))
    left = sub(left, mul(start_term, from_start))
    right = sub(right, mul(end_term, from_end))
    edge = jnp.stack((jnp.stack(left, 1), jnp.stack(right, 1)), 1)[:, :, :, None, :]

    back = pl.pallas_call(
        solve_kernel,
        grid=(blocks,),
        in_specs=[wide_block, seg_block, dev_block, mu_block, perm_block],
        out_specs=wide_block,
        out_shape=jax.ShapeDtypeStruct((vectors, fields, steps, modes), jnp.bfloat16),
        scratch_shapes=[
            pltpu.VMEM((2, steps, width), f32),
            pltpu.VMEM((2, steps, width), jnp.bfloat16),
        ],
        compiler_params=params,
        name="solve",
    )(zp, seg, edge, mu, perm.T)

    return jnp.einsum("rftj,sj->rfts", back, basis, preferred_element_type=jnp.float32)


def solution(mesh):
    placed = (P("grp", None, "tm", None), P("tm", None), P(), P())
    return jax.shard_map(
        on_device, mesh=mesh, in_specs=placed, out_specs=P("grp", None, "tm", None), check_vma=False
    )
```

```python
import functools

import jax
import jax.numpy as jnp
from jax import lax
from jax.experimental import pallas as pl
from jax.experimental.pallas import tpu as pltpu
from jax.sharding import PartitionSpec as P

SEGMENTS = 8


def mul(a, b):
    return a[0] * b[0] - a[1] * b[1], a[0] * b[1] + a[1] * b[0]


def add(a, b):
    return a[0] + b[0], a[1] + b[1]


def sub(a, b):
    return a[0] - b[0], a[1] - b[1]


def inverse_of(a):
    size = a[0] * a[0] + a[1] * a[1]
    return a[0] / size, -a[1] / size


def power(a, exponent):
    result, square = None, a
    while exponent:
        if exponent & 1:
            result = square if result is None else mul(result, square)
        exponent >>= 1
        if exponent:
            square = mul(square, square)
    return result


def decay_root(mu):
    wide = 2.0 + mu
    disc_re, disc_im = wide * wide - 5.0, -2.0 * wide
    size = jnp.sqrt(disc_re * disc_re + disc_im * disc_im)
    sqrt_re = jnp.sqrt(0.5 * (size + disc_re))
    sqrt_im = 0.5 * disc_im / sqrt_re
    half = inverse_of((wide + sqrt_re, sqrt_im - 1.0))
    return 2.0 * half[0], 2.0 * half[1]


def carries_kernel(modal_ref, mu_ref, perm_ref, zp_ref, seg_ref, dev_ref, z_ref):
    vectors, _, steps, width = modal_ref.shape
    per_seg = steps // SEGMENTS
    root = decay_root(mu_ref[...])
    root8 = tuple(jnp.broadcast_to(x, (SEGMENTS, width)) for x in root)
    jump = power(root, per_seg)
    for r in range(vectors):
        for f in range(2):
            rows = jnp.dot(perm_ref[...], modal_ref[r, f], preferred_element_type=jnp.float32)
            z_ref[r, f] = rows
            zp_ref[r, f] = rows.astype(jnp.bfloat16)
    for r in range(vectors):
        def at(k):
            here = pl.ds(k * SEGMENTS, SEGMENTS)
            return z_ref[r, 0, here, :], z_ref[r, 1, here, :]

        ahead, behind = at(0), at(per_seg - 1)
        for k in range(1, per_seg):
            ahead = add(at(k), mul(root8, ahead))
            behind = add(at(per_seg - 1 - k), mul(root8, behind))
        for c in range(2):
            seg_ref[r, 0, c] = ahead[c]
            seg_ref[r, 1, c] = behind[c]
        row = lambda a, s: (a[0][s:s + 1], a[1][s:s + 1])
        front, back = row(ahead, 0), row(behind, SEGMENTS - 1)
        for s in range(1, SEGMENTS):
            front = add(row(ahead, s), mul(jump, front))
            back = add(row(behind, SEGMENTS - 1 - s), mul(jump, back))
        for c in range(2):
            dev_ref[r, 0, c] = front[c]
            dev_ref[r, 1, c] = back[c]


def solve_kernel(zp_ref, seg_ref, edge_ref, mu_ref, perm_ref, out_ref, p_ref, u_ref):
    vectors, _, steps, width = zp_ref.shape
    per_seg = steps // SEGMENTS
    root = decay_root(mu_ref[...])
    root8 = tuple(jnp.broadcast_to(x, (SEGMENTS, width)) for x in root)
    jump = power(root, per_seg)
    square = mul(root, root)
    gain = mul(root, inverse_of((1.0 - square[0], -square[1])))
    for r in range(vectors):
        row = lambda a, s: (seg_ref[r, a, 0, s:s + 1, :], seg_ref[r, a, 1, s:s + 1, :])
        lefts = [(edge_ref[r, 0, 0], edge_ref[r, 0, 1])]
        rights = [(edge_ref[r, 1, 0], edge_ref[r, 1, 1])]
        for s in range(SEGMENTS):
            lefts.append(add(row(0, s), mul(jump, lefts[-1])))
        for s in range(SEGMENTS - 1, 0, -1):
            rights.append(add(row(1, s), mul(jump, rights[-1])))
        rights = rights[::-1]
        ends = [mul(gain, add(rights[s], mul(root, lefts[s + 1]))) for s in range(SEGMENTS)]
        stack = lambda rows: tuple(jnp.concatenate([x[c] for x in rows], axis=0) for c in range(2))
        p = stack(lefts[:SEGMENTS])
        for k in range(0, per_seg, 2):
            both = pl.ds(k * SEGMENTS, 2 * SEGMENTS)
            pair = [zp_ref[r, f, both, :].astype(jnp.float32) for f in range(2)]
            for h in range(2):
                z = tuple(x[h * SEGMENTS:(h + 1) * SEGMENTS] for x in pair)
                p = add(z, mul(root8, p))
                for c in range(2):
                    p_ref[c, pl.ds((k + h) * SEGMENTS, SEGMENTS), :] = p[c]
        u = stack(ends)
        for k in range(per_seg - 2, -1, -2):
            later = []
            for h in (1, 0):
                here = pl.ds((k + h) * SEGMENTS, SEGMENTS)
                u = mul(root8, add((p_ref[0, here, :], p_ref[1, here, :]), u))
                later.append(u)
            both = pl.ds(k * SEGMENTS, 2 * SEGMENTS)
            for c in range(2):
                u_ref[c, both, :] = jnp.concatenate([later[1][c], later[0][c]], axis=0).astype(jnp.bfloat16)
        for c in range(2):
            out_ref[r, c] = jnp.dot(perm_ref[...], u_ref[c], preferred_element_type=jnp.float32).astype(jnp.bfloat16)


def gather_kernel(chips, mine_ref, node_ref, out_ref, held, send_sem, recv_sem, pair_send, pair_recv):
    _, _, rows, modes = held.shape
    states = out_ref.shape[0]
    pieces = 4
    part = modes // pieces
    tile = min(512, states)
    me = lax.axis_index("tm")
    core, chip = me % 2, me // 2
    odd = chip % 2
    place = (1 - odd) * (chip // 2) + odd * (chips - 1 - chip // 2)

    def chip_at(position):
        position = (position + chips) % chips
        second = position // (chips // 2)
        return (1 - second) * 2 * position + second * (2 * (chips - 1 - position) + 1)

    targets = (chip_at(place + 1) * 2 + core, chip_at(place - 1) * 2 + core)
    pair = chip * 2 + 1 - core

    def piece(step, i):
        source = chip_at(place - step if i % 2 == 0 else place + step)
        return source, held.at[source, core, :, pl.ds(i * part, part)]

    def ring(step, i):
        _, ref = piece(step, i)
        return pltpu.make_async_remote_copy(
            src_ref=ref, dst_ref=ref, send_sem=send_sem.at[step, i], recv_sem=recv_sem.at[step, i],
            device_id={"tm": targets[i % 2]}, device_id_type=pl.DeviceIdType.MESH,
        )

    def landed(step, i):
        _, ref = piece(step + 1, i)
        return pltpu.make_async_remote_copy(
            src_ref=ref, dst_ref=ref, send_sem=send_sem.at[step, i], recv_sem=recv_sem.at[step, i],
            device_id={"tm": targets[i % 2]}, device_id_type=pl.DeviceIdType.MESH,
        )

    def share(step, i):
        _, ref = piece(step, i)
        return pltpu.make_async_remote_copy(
            src_ref=ref, dst_ref=ref, send_sem=pair_send.at[step, i], recv_sem=pair_recv.at[step, i],
            device_id={"tm": pair}, device_id_type=pl.DeviceIdType.MESH,
        )

    def place_rows(step, i, first):
        source, _ = piece(step, i)
        nodes = node_ref[source]
        columns = pl.ds(i * part, part)

        def one_tile(t, carry):
            start = pl.multiple_of(t * tile, tile)
            index = lax.broadcasted_iota(jnp.int32, (tile, 2 * rows), 0) + start
            choose = jnp.where(index == nodes, 1.0, 0.0).astype(jnp.bfloat16)
            block = held[source, :, :, columns].reshape(2 * rows, part)
            moved = jnp.dot(choose, block, preferred_element_type=jnp.float32)
            here = pl.ds(start, tile)
            if not first:
                moved = moved + out_ref[here, columns].astype(jnp.float32)
            out_ref[here, columns] = moved.astype(jnp.bfloat16)
            return carry

        lax.fori_loop(0, states // tile, one_tile, 0)

    held[chip, core] = mine_ref[...]
    barrier = pltpu.get_barrier_semaphore()
    for target in (*targets, pair):
        pl.semaphore_signal(barrier, inc=1, device_id={"tm": target}, device_id_type=pl.DeviceIdType.MESH)
    pl.semaphore_wait(barrier, 3)

    def one_step(step, first, last):
        for i in range(pieces):
            landed(step - 1, i).wait_recv()
            if not last:
                ring(step, i).start()
            share(step, i).start()
            share(step - 1, i).wait_recv()
            place_rows(step - 1, i, first)

    for i in range(pieces):
        ring(0, i).start()
        share(0, i).start()
    one_step(1, True, False)

    def body(step, carry):
        one_step(step, False, False)
        return carry

    lax.fori_loop(2, chips - 1, body, 0)
    one_step(chips - 1, False, True)
    for i in range(pieces):
        share(chips - 1, i).wait_recv()
        place_rows(chips - 1, i, False)

    def drain(step, carry):
        for i in range(pieces):
            ring(step, i).wait_send()
            share(step, i).wait_send()
        return carry

    lax.fori_loop(0, chips - 1, drain, 0)
    for i in range(pieces):
        share(chips - 1, i).wait_send()


def on_device(residual, eigenbasis, eigenvalues, node_order):
    vectors, fields, steps, states = residual.shape
    modes = eigenbasis.shape[1]
    parts = lax.axis_size("tm")
    me = lax.axis_index("tm")
    per_seg = steps // SEGMENTS
    width = min(256, modes)
    blocks = modes // width

    chips = parts // 2
    rows = eigenbasis.shape[0]
    basis = pl.pallas_call(
        functools.partial(gather_kernel, chips),
        out_shape=jax.ShapeDtypeStruct((states, modes), jnp.bfloat16),
        in_specs=[pl.BlockSpec(memory_space=pltpu.VMEM)] * 2,
        out_specs=pl.BlockSpec(memory_space=pltpu.VMEM),
        scratch_shapes=[pltpu.VMEM((chips, 2, rows, modes), jnp.bfloat16)]
        + [pltpu.SemaphoreType.DMA((chips, 4))] * 4,
        compiler_params=pltpu.CompilerParams(
            collective_id=0, has_side_effects=True, vmem_limit_bytes=44 * 1024 * 1024
        ),
        name="gather_rows",
    )(eigenbasis, node_order.reshape(chips, 1, 2 * rows))

    modal = jnp.einsum("rfts,sj->rftj", residual, basis, preferred_element_type=jnp.float32).astype(jnp.bfloat16)

    row = jnp.arange(steps, dtype=jnp.int32)
    time_of_row = (row % SEGMENTS) * per_seg + row // SEGMENTS
    perm = (time_of_row[:, None] == row[None, :]).astype(jnp.bfloat16)
    mu = eigenvalues[None, :]

    f32 = jnp.float32
    wide_block = pl.BlockSpec((vectors, fields, steps, width), lambda j: (0, 0, 0, j))
    seg_block = pl.BlockSpec((vectors, 2, 2, SEGMENTS, width), lambda j: (0, 0, 0, 0, j))
    dev_block = pl.BlockSpec((vectors, 2, 2, 1, width), lambda j: (0, 0, 0, 0, j))
    mu_block = pl.BlockSpec((1, width), lambda j: (0, j))
    perm_block = pl.BlockSpec((steps, steps), lambda j: (0, 0))
    params = pltpu.CompilerParams(vmem_limit_bytes=40 * 1024 * 1024)
    zp, seg, dev = pl.pallas_call(
        carries_kernel,
        grid=(blocks,),
        in_specs=[wide_block, mu_block, perm_block],
        out_specs=[wide_block, seg_block, dev_block],
        out_shape=[
            jax.ShapeDtypeStruct((vectors, fields, steps, modes), jnp.bfloat16),
            jax.ShapeDtypeStruct((vectors, 2, 2, SEGMENTS, modes), f32),
            jax.ShapeDtypeStruct((vectors, 2, 2, 1, modes), f32),
        ],
        scratch_shapes=[pltpu.VMEM((vectors, fields, steps, width), f32)],
        compiler_params=params,
        name="carries",
    )(modal, mu, perm)

    root = decay_root(mu)
    hop = power(root, steps)
    one = (jnp.ones_like(mu), jnp.zeros_like(mu))
    zero = (jnp.zeros((vectors, modes), f32),) * 2
    pick = lambda keep, new, old: tuple(jnp.where(keep, a, b) for a, b in zip(new, old))
    group = dev[:, :, :, 0, :]
    left, right = zero, zero
    from_start, from_end, span, reach = one, one, hop, 1
    while reach < parts:
        other = lax.ppermute(group, "tm", [(d, d ^ reach) for d in range(parts)])
        upper = (me // reach) % 2 == 1
        low, high = jnp.where(upper, other, group), jnp.where(upper, group, other)
        low_front, high_front = (low[:, 0, 0], low[:, 0, 1]), (high[:, 0, 0], high[:, 0, 1])
        low_back, high_back = (low[:, 1, 0], low[:, 1, 1]), (high[:, 1, 0], high[:, 1, 1])
        left = pick(upper, add(left, mul(from_start, low_front)), left)
        right = pick(upper, right, add(right, mul(from_end, high_back)))
        from_start = pick(upper, mul(from_start, span), from_start)
        from_end = pick(upper, from_end, mul(from_end, span))
        front, back = add(high_front, mul(span, low_front)), add(low_back, mul(span, high_back))
        group = jnp.stack((jnp.stack(front, 1), jnp.stack(back, 1)), 1)
        span, reach = mul(span, span), 2 * reach
    all_left, all_right = (group[:, 0, 0], group[:, 0, 1]), (group[:, 1, 0], group[:, 1, 1])
    whole = mul(span, root)
    whole_sq = mul(whole, whole)
    scale = mul(root, inverse_of((1.0 - whole_sq[0], -whole_sq[1])))
    start_term = mul(scale, sub(all_right, mul(whole, all_left)))
    end_term = mul(scale, sub(all_left, mul(whole, all_right)))
    left = sub(left, mul(start_term, from_start))
    right = sub(right, mul(end_term, from_end))
    edge = jnp.stack((jnp.stack(left, 1), jnp.stack(right, 1)), 1)[:, :, :, None, :]

    back = pl.pallas_call(
        solve_kernel,
        grid=(blocks,),
        in_specs=[wide_block, seg_block, dev_block, mu_block, perm_block],
        out_specs=wide_block,
        out_shape=jax.ShapeDtypeStruct((vectors, fields, steps, modes), jnp.bfloat16),
        scratch_shapes=[
            pltpu.VMEM((2, steps, width), f32),
            pltpu.VMEM((2, steps, width), jnp.bfloat16),
        ],
        compiler_params=params,
        name="solve",
    )(zp, seg, edge, mu, perm.T)

    return jnp.einsum("rftj,sj->rfts", back, basis, preferred_element_type=jnp.float32)


def solution(mesh):
    placed = (P("grp", None, "tm", None), P("tm", None), P(), P())
    return jax.shard_map(
        on_device, mesh=mesh, in_specs=placed, out_specs=P("grp", None, "tm", None), check_vma=False
    )
```

```python
import functools

import jax
import jax.numpy as jnp
from jax import lax
from jax.experimental import pallas as pl
from jax.experimental.pallas import tpu as pltpu
from jax.sharding import PartitionSpec as P

SEGMENTS = 8


def mul(a, b):
    return a[0] * b[0] - a[1] * b[1], a[0] * b[1] + a[1] * b[0]


def add(a, b):
    return a[0] + b[0], a[1] + b[1]


def sub(a, b):
    return a[0] - b[0], a[1] - b[1]


def inverse_of(a):
    size = a[0] * a[0] + a[1] * a[1]
    return a[0] / size, -a[1] / size


def power(a, exponent):
    result, square = None, a
    while exponent:
        if exponent & 1:
            result = square if result is None else mul(result, square)
        exponent >>= 1
        if exponent:
            square = mul(square, square)
    return result


def decay_root(mu):
    wide = 2.0 + mu
    disc_re, disc_im = wide * wide - 5.0, -2.0 * wide
    size = jnp.sqrt(disc_re * disc_re + disc_im * disc_im)
    sqrt_re = jnp.sqrt(0.5 * (size + disc_re))
    sqrt_im = 0.5 * disc_im / sqrt_re
    half = inverse_of((wide + sqrt_re, sqrt_im - 1.0))
    return 2.0 * half[0], 2.0 * half[1]


def carries_kernel(modal_ref, mu_ref, perm_ref, zp_ref, seg_ref, dev_ref, z_ref):
    vectors, _, steps, width = modal_ref.shape
    per_seg = steps // SEGMENTS
    root = decay_root(mu_ref[...])
    root8 = tuple(jnp.broadcast_to(x, (SEGMENTS, width)) for x in root)
    jump = power(root, per_seg)
    for r in range(vectors):
        for f in range(2):
            rows = jnp.dot(perm_ref[...], modal_ref[r, f], preferred_element_type=jnp.float32)
            z_ref[r, f] = rows
            zp_ref[r, f] = rows.astype(jnp.bfloat16)
    for r in range(vectors):
        def at(k):
            here = pl.ds(k * SEGMENTS, SEGMENTS)
            return z_ref[r, 0, here, :], z_ref[r, 1, here, :]

        ahead, behind = at(0), at(per_seg - 1)
        for k in range(1, per_seg):
            ahead = add(at(k), mul(root8, ahead))
            behind = add(at(per_seg - 1 - k), mul(root8, behind))
        for c in range(2):
            seg_ref[r, 0, c] = ahead[c]
            seg_ref[r, 1, c] = behind[c]
        row = lambda a, s: (a[0][s:s + 1], a[1][s:s + 1])
        front, back = row(ahead, 0), row(behind, SEGMENTS - 1)
        for s in range(1, SEGMENTS):
            front = add(row(ahead, s), mul(jump, front))
            back = add(row(behind, SEGMENTS - 1 - s), mul(jump, back))
        for c in range(2):
            dev_ref[r, 0, c] = front[c]
            dev_ref[r, 1, c] = back[c]


def solve_kernel(zp_ref, seg_ref, edge_ref, mu_ref, perm_ref, out_ref, p_ref, u_ref):
    vectors, _, steps, width = zp_ref.shape
    per_seg = steps // SEGMENTS
    root = decay_root(mu_ref[...])
    root8 = tuple(jnp.broadcast_to(x, (SEGMENTS, width)) for x in root)
    jump = power(root, per_seg)
    square = mul(root, root)
    gain = mul(root, inverse_of((1.0 - square[0], -square[1])))
    for r in range(vectors):
        row = lambda a, s: (seg_ref[r, a, 0, s:s + 1, :], seg_ref[r, a, 1, s:s + 1, :])
        lefts = [(edge_ref[r, 0, 0], edge_ref[r, 0, 1])]
        rights = [(edge_ref[r, 1, 0], edge_ref[r, 1, 1])]
        for s in range(SEGMENTS):
            lefts.append(add(row(0, s), mul(jump, lefts[-1])))
        for s in range(SEGMENTS - 1, 0, -1):
            rights.append(add(row(1, s), mul(jump, rights[-1])))
        rights = rights[::-1]
        ends = [mul(gain, add(rights[s], mul(root, lefts[s + 1]))) for s in range(SEGMENTS)]
        stack = lambda rows: tuple(jnp.concatenate([x[c] for x in rows], axis=0) for c in range(2))
        p = stack(lefts[:SEGMENTS])
        for k in range(0, per_seg, 2):
            both = pl.ds(k * SEGMENTS, 2 * SEGMENTS)
            pair = [zp_ref[r, f, both, :].astype(jnp.float32) for f in range(2)]
            for h in range(2):
                z = tuple(x[h * SEGMENTS:(h + 1) * SEGMENTS] for x in pair)
                p = add(z, mul(root8, p))
                for c in range(2):
                    p_ref[c, pl.ds((k + h) * SEGMENTS, SEGMENTS), :] = p[c]
        u = stack(ends)
        for k in range(per_seg - 2, -1, -2):
            later = []
            for h in (1, 0):
                here = pl.ds((k + h) * SEGMENTS, SEGMENTS)
                u = mul(root8, add((p_ref[0, here, :], p_ref[1, here, :]), u))
                later.append(u)
            both = pl.ds(k * SEGMENTS, 2 * SEGMENTS)
            for c in range(2):
                u_ref[c, both, :] = jnp.concatenate([later[1][c], later[0][c]], axis=0).astype(jnp.bfloat16)
        for c in range(2):
            out_ref[r, c] = jnp.dot(perm_ref[...], u_ref[c], preferred_element_type=jnp.float32).astype(jnp.bfloat16)


def gather_kernel(chips, mine_ref, node_ref, out_ref, held, send_sem, recv_sem, pair_send, pair_recv):
    _, _, rows, modes = held.shape
    states = out_ref.shape[0]
    pieces = 4
    part = modes // pieces
    tile = min(512, states)
    me = lax.axis_index("tm")
    core, chip = me % 2, me // 2
    odd = chip % 2
    place = (1 - odd) * (chip // 2) + odd * (chips - 1 - chip // 2)

    def chip_at(position):
        position = (position + chips) % chips
        second = position // (chips // 2)
        return (1 - second) * 2 * position + second * (2 * (chips - 1 - position) + 1)

    targets = (chip_at(place + 1) * 2 + core, chip_at(place - 1) * 2 + core)
    pair = chip * 2 + 1 - core

    def piece(step, i):
        source = chip_at(place - step if i % 2 == 0 else place + step)
        return source, held.at[source, core, :, pl.ds(i * part, part)]

    def ring(step, i):
        _, ref = piece(step, i)
        return pltpu.make_async_remote_copy(
            src_ref=ref, dst_ref=ref, send_sem=send_sem.at[step, i], recv_sem=recv_sem.at[step, i],
            device_id={"tm": targets[i % 2]}, device_id_type=pl.DeviceIdType.MESH,
        )

    def landed(step, i):
        _, ref = piece(step + 1, i)
        return pltpu.make_async_remote_copy(
            src_ref=ref, dst_ref=ref, send_sem=send_sem.at[step, i], recv_sem=recv_sem.at[step, i],
            device_id={"tm": targets[i % 2]}, device_id_type=pl.DeviceIdType.MESH,
        )

    def share(step, i):
        _, ref = piece(step, i)
        return pltpu.make_async_remote_copy(
            src_ref=ref, dst_ref=ref, send_sem=pair_send.at[step, i], recv_sem=pair_recv.at[step, i],
            device_id={"tm": pair}, device_id_type=pl.DeviceIdType.MESH,
        )

    def place_rows(step, i, first):
        if i < 2:
            return
        source, _ = piece(step, i)
        nodes = node_ref[source]

        def one_tile(t, carry):
            start = pl.multiple_of(t * tile, tile)
            index = lax.broadcasted_iota(jnp.int32, (tile, 2 * rows), 0) + start
            choose = jnp.where(index == nodes, 1.0, 0.0).astype(jnp.bfloat16)
            here = pl.ds(start, tile)
            for c in (i - 2, i):
                columns = pl.ds(c * part, part)
                block = held[source, :, :, columns].reshape(2 * rows, part)
                moved = jnp.dot(choose, block, preferred_element_type=jnp.float32).astype(jnp.bfloat16)
                out_ref[here, columns] = moved if first else moved + out_ref[here, columns]
            return carry

        lax.fori_loop(0, states // tile, one_tile, 0)

    held[chip, core] = mine_ref[...]
    barrier = pltpu.get_barrier_semaphore()
    for target in (*targets, pair):
        pl.semaphore_signal(barrier, inc=1, device_id={"tm": target}, device_id_type=pl.DeviceIdType.MESH)
    pl.semaphore_wait(barrier, 3)

    def one_step(step, first, last):
        for i in range(pieces):
            landed(step - 1, i).wait_recv()
            if not last:
                ring(step, i).start()
            share(step, i).start()
            share(step - 1, i).wait_recv()
            place_rows(step - 1, i, first)

    for i in range(pieces):
        ring(0, i).start()
        share(0, i).start()
    one_step(1, True, False)

    def body(step, carry):
        one_step(step, False, False)
        return carry

    lax.fori_loop(2, chips - 1, body, 0)
    one_step(chips - 1, False, True)
    for i in range(pieces):
        share(chips - 1, i).wait_recv()
        place_rows(chips - 1, i, False)

    def drain(step, carry):
        for i in range(pieces):
            ring(step, i).wait_send()
            share(step, i).wait_send()
        return carry

    lax.fori_loop(0, chips - 1, drain, 0)
    for i in range(pieces):
        share(chips - 1, i).wait_send()


def on_device(residual, eigenbasis, eigenvalues, node_order):
    vectors, fields, steps, states = residual.shape
    modes = eigenbasis.shape[1]
    parts = lax.axis_size("tm")
    me = lax.axis_index("tm")
    per_seg = steps // SEGMENTS
    width = min(256, modes)
    blocks = modes // width

    chips = parts // 2
    rows = eigenbasis.shape[0]
    basis = pl.pallas_call(
        functools.partial(gather_kernel, chips),
        out_shape=jax.ShapeDtypeStruct((states, modes), jnp.bfloat16),
        in_specs=[pl.BlockSpec(memory_space=pltpu.VMEM)] * 2,
        out_specs=pl.BlockSpec(memory_space=pltpu.VMEM),
        scratch_shapes=[pltpu.VMEM((chips, 2, rows, modes), jnp.bfloat16)]
        + [pltpu.SemaphoreType.DMA((chips, 4))] * 4,
        compiler_params=pltpu.CompilerParams(
            collective_id=0, has_side_effects=True, vmem_limit_bytes=44 * 1024 * 1024
        ),
        name="gather_rows",
    )(eigenbasis, node_order.reshape(chips, 1, 2 * rows))

    modal = jnp.einsum("rfts,sj->rftj", residual, basis, preferred_element_type=jnp.float32).astype(jnp.bfloat16)

    row = jnp.arange(steps, dtype=jnp.int32)
    time_of_row = (row % SEGMENTS) * per_seg + row // SEGMENTS
    perm = (time_of_row[:, None] == row[None, :]).astype(jnp.bfloat16)
    mu = eigenvalues[None, :]

    f32 = jnp.float32
    wide_block = pl.BlockSpec((vectors, fields, steps, width), lambda j: (0, 0, 0, j))
    seg_block = pl.BlockSpec((vectors, 2, 2, SEGMENTS, width), lambda j: (0, 0, 0, 0, j))
    dev_block = pl.BlockSpec((vectors, 2, 2, 1, width), lambda j: (0, 0, 0, 0, j))
    mu_block = pl.BlockSpec((1, width), lambda j: (0, j))
    perm_block = pl.BlockSpec((steps, steps), lambda j: (0, 0))
    params = pltpu.CompilerParams(vmem_limit_bytes=40 * 1024 * 1024)
    zp, seg, dev = pl.pallas_call(
        carries_kernel,
        grid=(blocks,),
        in_specs=[wide_block, mu_block, perm_block],
        out_specs=[wide_block, seg_block, dev_block],
        out_shape=[
            jax.ShapeDtypeStruct((vectors, fields, steps, modes), jnp.bfloat16),
            jax.ShapeDtypeStruct((vectors, 2, 2, SEGMENTS, modes), f32),
            jax.ShapeDtypeStruct((vectors, 2, 2, 1, modes), f32),
        ],
        scratch_shapes=[pltpu.VMEM((vectors, fields, steps, width), f32)],
        compiler_params=params,
        name="carries",
    )(modal, mu, perm)

    root = decay_root(mu)
    hop = power(root, steps)
    one = (jnp.ones_like(mu), jnp.zeros_like(mu))
    zero = (jnp.zeros((vectors, modes), f32),) * 2
    pick = lambda keep, new, old: tuple(jnp.where(keep, a, b) for a, b in zip(new, old))
    group = dev[:, :, :, 0, :]
    left, right = zero, zero
    from_start, from_end, span, reach = one, one, hop, 1
    while reach < parts:
        other = lax.ppermute(group, "tm", [(d, d ^ reach) for d in range(parts)])
        upper = (me // reach) % 2 == 1
        low, high = jnp.where(upper, other, group), jnp.where(upper, group, other)
        low_front, high_front = (low[:, 0, 0], low[:, 0, 1]), (high[:, 0, 0], high[:, 0, 1])
        low_back, high_back = (low[:, 1, 0], low[:, 1, 1]), (high[:, 1, 0], high[:, 1, 1])
        left = pick(upper, add(left, mul(from_start, low_front)), left)
        right = pick(upper, right, add(right, mul(from_end, high_back)))
        from_start = pick(upper, mul(from_start, span), from_start)
        from_end = pick(upper, from_end, mul(from_end, span))
        front, back = add(high_front, mul(span, low_front)), add(low_back, mul(span, high_back))
        group = jnp.stack((jnp.stack(front, 1), jnp.stack(back, 1)), 1)
        span, reach = mul(span, span), 2 * reach
    all_left, all_right = (group[:, 0, 0], group[:, 0, 1]), (group[:, 1, 0], group[:, 1, 1])
    whole = mul(span, root)
    whole_sq = mul(whole, whole)
    scale = mul(root, inverse_of((1.0 - whole_sq[0], -whole_sq[1])))
    start_term = mul(scale, sub(all_right, mul(whole, all_left)))
    end_term = mul(scale, sub(all_left, mul(whole, all_right)))
    left = sub(left, mul(start_term, from_start))
    right = sub(right, mul(end_term, from_end))
    edge = jnp.stack((jnp.stack(left, 1), jnp.stack(right, 1)), 1)[:, :, :, None, :]

    back = pl.pallas_call(
        solve_kernel,
        grid=(blocks,),
        in_specs=[wide_block, seg_block, dev_block, mu_block, perm_block],
        out_specs=wide_block,
        out_shape=jax.ShapeDtypeStruct((vectors, fields, steps, modes), jnp.bfloat16),
        scratch_shapes=[
            pltpu.VMEM((2, steps, width), f32),
            pltpu.VMEM((2, steps, width), jnp.bfloat16),
        ],
        compiler_params=params,
        name="solve",
    )(zp, seg, edge, mu, perm.T)

    return jnp.einsum("rftj,sj->rfts", back, basis, preferred_element_type=jnp.float32)


def solution(mesh):
    placed = (P("grp", None, "tm", None), P("tm", None), P(), P())
    return jax.shard_map(
        on_device, mesh=mesh, in_specs=placed, out_specs=P("grp", None, "tm", None), check_vma=False
    )
```
